32 devices in a mesh: tile: 16 (over z, x, core), harm: 2 (over y).
Axes of the slice: x: 2, y: 2, z: 4, core: 2. Of those that a mesh axis runs over, the one named last changes fastest.
Arguments:
- adjoint: float32 [24, 64, 320], P('harm', 'tile'), may hold values from -6 to 6
- objective_grad: float32 [24, 64, 320], P('harm', 'tile'), may hold values from -6 to 6
- first_jacobian_blocks: bfloat16 [64, 4, 320, 320], P(('tile', 'harm')), may hold values from -0.15625 to 0.15625
- second_jacobian_blocks: bfloat16 [64, 4, 320, 320], P(('tile', 'harm')), may hold values from -0.15625 to 0.15625
- block_column_layout: int32 [64, 4], P('tile'), may hold values from 0 to 11
- coupling: float32 [24, 24], replicated, may hold values from -1.25 to 1.25
- matching: int32 [64, 2], P('tile'), may hold values from 0 to 3
- intersection: float32 [64, 2], P('tile'), may hold values from 0.25 to 1
- modes: int32 [12], replicated, may hold values from -6 to 6
- clocking: float32 [64], P('tile'), may hold values from -3.140625 to 3.140625
Outputs:
- update: float32 [24, 64, 320], P('harm', 'tile')
The draws below stay inside these ranges and needn't reach their ends.
All inputs are finite; a program needn't handle non-finite values.
Results may differ from the reference program's by a relative error of at most 0.0033.
Values may be sent and summed in bfloat16 or wider, within the bound.
A program may use at most 128 MiB of HBM per device.

```python
import jax
import jax.numpy as jnp
from jax import lax

NH = 12
HC = 24
CV = 320
SW = 40
K = 4
TD = 4
NT = 64


def with_ends(entries, key, low, largest):
    longest = entries.shape.index(max(entries.shape))
    spots = []
    for shift in (0, 1):
        where = [jax.random.randint(jax.random.fold_in(key, axis), (), 0, length) for axis, length in enumerate(entries.shape)]
        where[longest] = (where[longest] + shift) % entries.shape[longest]
        spots.append(tuple(where))
    return entries.at[spots[0]].set(low).at[spots[1]].set(largest)


def shard_levels(stream_key, shape, shards, least, high):
    def one(dim, parts):
        draws = jax.random.uniform(jax.random.fold_in(jax.random.fold_in(stream_key, 6), dim), (parts,), jnp.float32, least / len(shards), high / len(shards))
        return jnp.repeat(jnp.exp(draws), shape[dim] // parts).reshape((-1,) + (1,) * (len(shape) - dim - 1))

    factor_of = one(*shards[0])
    for cut in shards[1:]:
        factor_of = factor_of * one(*cut)
    return factor_of


def scatter_about(own_key, extent, deviation, limit, shards=(), held_as=jnp.bfloat16):
    result = jax.random.normal(own_key, extent, jnp.float32) * deviation
    if len(shards) > 0:
        result = shard_levels(own_key, extent, shards, -0.22, 0.18) * result
    return jnp.clip(result, min=-limit, max=limit).astype(held_as)


def setup_inputs(seed: int = 0) -> dict:
    streams_of = jax.random.split(jax.random.key(seed), 11)
    return {
        "adjoint": scatter_about(streams_of[0], (HC, NT, CV), 1.0, 6.0, ((0, 2), (1, 16)), jnp.float32),
        "objective_grad": scatter_about(streams_of[1], (HC, NT, CV), 1.0, 6.0, ((0, 2), (1, 16)), jnp.float32),
        "first_jacobian_blocks": scatter_about(streams_of[2], (NT, K, CV, CV), (CV * K) ** -0.5, 0.15625, ((0, 32),)),
        "second_jacobian_blocks": scatter_about(streams_of[3], (NT, K, CV, CV), (CV * K) ** -0.5, 0.15625, ((0, 32),)),
        "block_column_layout": with_ends(jax.random.randint(streams_of[4], (NT, K), 0, 3 * TD), jax.random.fold_in(streams_of[4], 1), 0, (3 * TD) - 1).astype(jnp.int32),
        "coupling": scatter_about(streams_of[5], (HC, HC), HC ** -0.5, 1.25, (), jnp.float32),
        "matching": with_ends(jax.random.randint(streams_of[6], (NT, 2), 0, TD), jax.random.fold_in(streams_of[6], 1), 0, TD - 1).astype(jnp.int32),
        "intersection": jnp.clip(0.25 + 0.75 * jax.random.uniform(streams_of[7], (NT, 2), jnp.float32) ** shard_levels(streams_of[7], (NT, 2), ((0, 16),), -0.2, 0.2), 0.25, 1.0),
        "modes": with_ends(jax.random.randint(streams_of[8], (NH,), -6, 7), jax.random.fold_in(streams_of[8], 1), -6, 6).astype(jnp.int32),
        "clocking": jnp.clip(jax.random.uniform(streams_of[9], (NT,), jnp.float32, -3.140625, 3.140625), -3.140625, 3.140625),
    }


def sparse_block_product(jacobian_blocks, vector_batch, sparsity_layout):
    tiles = jnp.arange(NT, dtype=jnp.int32)
    cols = ((tiles - tiles % TD - TD)[:, None] + sparsity_layout) % NT

    def one_tile(args):
        block, vec = args
        return jnp.einsum("hc,kcd->khd", vec.astype(jnp.float32), block.astype(jnp.float32), precision=lax.Precision.HIGHEST)

    term_list = lax.map(one_tile, (jacobian_blocks, jnp.transpose(vector_batch, (1, 0, 2))))
    summed = jax.ops.segment_sum(term_list.reshape(NT * K, HC, CV), cols.reshape(-1).astype(jnp.int32), num_segments=NT)
    return jnp.transpose(summed, (1, 0, 2))


def reference(adjoint, objective_grad, first_jacobian_blocks, second_jacobian_blocks, block_column_layout, coupling, matching, intersection, modes, clocking):
    adjoint_batch = adjoint.astype(jnp.bfloat16)
    first_operator = sparse_block_product(first_jacobian_blocks, adjoint_batch, block_column_layout)
    tiles = jnp.arange(NT, dtype=jnp.int32)
    partner_side = ((tiles - tiles % TD + NT // 2) % NT)[:, None] + matching
    strips = first_operator[:, :, :SW]
    mortar_coupling = intersection[None, :, 0, None] * strips[:, partner_side[:, 0], :] + intersection[None, :, 1, None] * strips[:, partner_side[:, 1], :]
    phi = modes.astype(jnp.float32)[:, None] * clocking[None, :]
    cosine = jnp.cos(phi)[:, :, None]
    sine = jnp.sin(phi)[:, :, None]
    mortar_cos = mortar_coupling[:NH]
    mortar_sin = mortar_coupling[NH:]
    rotated = jnp.concatenate([cosine * mortar_cos - sine * mortar_sin, sine * mortar_cos + cosine * mortar_sin], axis=0)
    mixed = jnp.einsum("hg,gtd->htd", coupling, first_operator, precision=lax.Precision.HIGHEST)
    padded = jnp.pad(rotated, ((0, 0), (0, 0), (0, CV - SW)))
    coupled_result = (first_operator + mixed + padded).astype(jnp.bfloat16)
    second_operator = sparse_block_product(second_jacobian_blocks, coupled_result, block_column_layout)
    return objective_grad - second_operator
```

```python
import functools

import jax
import jax.numpy as jnp
from jax import lax
from jax.experimental import pallas as pl
from jax.experimental.pallas import tpu as pltpu
from jax.sharding import PartitionSpec as P

VARS = 5
IF_CELLS = 8
STRIP = VARS * IF_CELLS
LANES = 128
MESH = pl.DeviceIdType.MESH


def kernel(
    tiles,
    harms,
    adj,
    layout,
    coupling,
    matching,
    weights,
    modes,
    clocking,
    first_hbm,
    second_hbm,
    out,
    first_j,
    second_j,
    pad,
    a_send,
    a_recv,
    full,
    terms,
    send1,
    recv1,
    m_send,
    m_recv,
    swap,
    send2,
    recv2,
    j1_sem,
    j2_sem,
    a_ssem,
    a_rsem,
    s1_sem,
    r1_sem,
    m_ssem,
    m_rsem,
    s2_sem,
    r2_sem,
):
    my_t = lax.axis_index("tile")
    my_h = lax.axis_index("harm")
    own_hc, group, width = adj.shape
    rows, kk = first_j.shape[0], first_j.shape[1]
    hc = coupling.shape[0]
    half = hc // 2
    base = my_h * rows
    far = lax.rem(my_t + tiles // 2, tiles)
    near = [lax.rem(my_t + tiles - 1, tiles), my_t, lax.rem(my_t + 1, tiles)]

    def block_copies(hbm, vmem, sem):
        return [
            pltpu.make_async_copy(hbm.at[r, k], vmem.at[r, k], sem.at[r * kk + k])
            for r in range(rows)
            for k in range(kk)
        ]

    first_copies = block_copies(first_hbm, first_j, j1_sem)
    second_copies = block_copies(second_hbm, second_j, j2_sem)
    for copy in first_copies:
        copy.start()

    barrier = pltpu.get_barrier_semaphore()
    for d in (-1, 0, 1):
        for h in range(harms):
            if d == 0:
                @pl.when(h != my_h)
                def _():
                    pl.semaphore_signal(barrier, inc=1, device_id=(my_t, h), device_id_type=MESH)
            else:
                pl.semaphore_signal(barrier, inc=1, device_id=(near[d + 1], h), device_id_type=MESH)
    for h in range(harms):
        pl.semaphore_signal(barrier, inc=1, device_id=(far, h), device_id_type=MESH)

    pad[...] = jnp.zeros_like(pad)
    for h in range(harms):
        for r in range(rows):
            pad[h * rows + r, 0:own_hc, :] = adj[:, h * rows + r, :]
    for h in range(harms):
        for r in range(rows):
            a_send[h, r] = pad[h * rows + r].astype(jnp.bfloat16)

    pl.semaphore_wait(barrier, 4 * harms - 1)

    def a_copy(to, slot, sem):
        return pltpu.make_async_remote_copy(
            src_ref=a_send.at[to],
            dst_ref=a_recv.at[slot],
            send_sem=a_ssem.at[to],
            recv_sem=a_rsem.at[sem],
            device_id=(my_t, to),
            device_id_type=MESH,
        )

    def other(h):
        return h != my_h

    for h in range(harms):
        @pl.when(other(h))
        def _():
            a_copy(h, my_h, my_h).start()

    for copy in second_copies:
        copy.start()

    a_recv[my_h] = a_send[my_h]

    row_id = lax.broadcasted_iota(jnp.int32, (hc, LANES), 0)
    lane_id = lax.broadcasted_iota(jnp.int32, (hc, LANES), 1)
    mode = jnp.zeros((hc, LANES), jnp.float32)
    for n in range(half):
        value = modes[n].astype(jnp.float32)
        mode = jnp.where((row_id == n) | (row_id == n + half), value, mode)
    cosines, sines = [], []
    for r in range(rows):
        phi = mode * clocking[base + r]
        inside = lane_id < STRIP
        sine = jnp.sin(phi)
        cosines.append(jnp.where(inside, jnp.cos(phi), 0.0))
        sines.append(jnp.where(inside, jnp.where(row_id < half, -sine, sine), 0.0))

    spot = [[layout[base + r, k] for k in range(kk)] for r in range(rows)]

    def one(r, k, slot):
        return jnp.where(spot[r][k] == slot, 1.0, 0.0).astype(jnp.float32)

    def fold(slot):
        total = None
        for r in range(rows):
            for k in range(kk):
                term = one(r, k, slot) * terms[r * kk + k]
                total = term if total is None else total + term
        return total

    for h in range(harms):
        @pl.when(other(h))
        def _():
            a_copy(h, h, h).wait_recv()
    for r in range(rows):
        for h in range(harms):
            full[r, h * own_hc : (h + 1) * own_hc, :] = a_recv[h, r].astype(jnp.float32)[0:own_hc]

    def products(vectors, blocks, copies):
        for r in range(rows):
            for k in range(kk):
                copies[r * kk + k].wait()
                terms[r * kk + k] = jnp.dot(
                    vectors[r], blocks[r, k], preferred_element_type=jnp.float32
                )

    def exchange(send, recv, ssem, rsem):
        def copy(d, to, slot):
            return pltpu.make_async_remote_copy(
                src_ref=send.at[(d + 1) * harms + to],
                dst_ref=recv.at[slot],
                send_sem=ssem.at[(d + 1) * harms + to],
                recv_sem=rsem.at[slot],
                device_id=(near[d + 1], to),
                device_id_type=MESH,
            )

        def start(d, to):
            if d == 0:
                @pl.when(other(to))
                def _():
                    copy(d, to, harms + my_h).start()
            else:
                copy(d, to, (d + 1) * harms + my_h).start()

        def finish(d, h):
            if d == 0:
                @pl.when(other(h))
                def _():
                    copy(d, h, harms + h).wait_recv()
            else:
                copy(d, h, (d + 1) * harms + h).wait_recv()

        def drain():
            for d in (-1, 0, 1):
                for h in range(harms):
                    if d == 0:
                        @pl.when(other(h))
                        def _():
                            copy(d, h, harms + h).wait_send()
                    else:
                        copy(d, h, (d + 1) * harms + h).wait_send()

        def collect():
            total = send[harms + my_h]
            for d in (-1, 1, 0):
                for h in range(harms):
                    finish(d, h)
                if d == 0:
                    for j in range(1, harms):
                        total = total + recv[harms + lax.rem(my_h + j, harms)]
                else:
                    for h in range(harms):
                        total = total + recv[(d + 1) * harms + h]
            return total

        return start, collect, drain

    start1, collect1, drain1 = exchange(send1, recv1, s1_sem, r1_sem)
    start2, collect2, drain2 = exchange(send2, recv2, s2_sem, r2_sem)

    products([full[r].astype(jnp.bfloat16) for r in range(rows)], first_j, first_copies)
    for d in (-1, 1, 0):
        for h in range(harms):
            for r in range(rows):
                send1[(d + 1) * harms + h, r] = fold((d + 1) * group + h * rows + r)
            start1(d, h)
    first = collect1()

    m_send[...] = first[:, :, 0:LANES]

    def m_copy(to, slot):
        return pltpu.make_async_remote_copy(
            src_ref=m_send,
            dst_ref=m_recv.at[slot],
            send_sem=m_ssem.at[to],
            recv_sem=m_rsem.at[slot],
            device_id=(far, to),
            device_id_type=MESH,
        )

    for h in range(harms):
        m_copy(h, my_h).start()
    plain = []
    for r in range(rows):
        plain.append(
            first[r]
            + jnp.dot(
                coupling[...],
                first[r],
                precision=lax.Precision.HIGHEST,
                preferred_element_type=jnp.float32,
            )
        )
    for h in range(harms):
        m_copy(h, h).wait_recv()
    coupled = []
    for r in range(rows):
        mortar = jnp.zeros((hc, LANES), jnp.float32)
        for h in range(harms):
            for q in range(rows):
                place = h * rows + q
                weight = jnp.where(matching[base + r, 0] == place, weights[base + r, 0], 0.0)
                weight = weight + jnp.where(matching[base + r, 1] == place, weights[base + r, 1], 0.0)
                mortar = mortar + weight * m_recv[h, q]
        swap[r, 0:half, :] = mortar[half:]
        swap[r, half:, :] = mortar[0:half]
        rotated = cosines[r] * mortar + sines[r] * swap[r]
        head = plain[r][:, 0:LANES] + rotated
        coupled.append(
            jnp.concatenate([head, plain[r][:, LANES:]], axis=1).astype(jnp.bfloat16)
        )

    products(coupled, second_j, second_copies)
    for d in (-1, 1, 0):
        for s in range(group):
            value = fold((d + 1) * group + s)
            for h in range(harms):
                send2[(d + 1) * harms + h, s * own_hc : (s + 1) * own_hc, :] = value[
                    h * own_hc : (h + 1) * own_hc
                ]
        for h in range(harms):
            start2(d, h)
    out[...] = collect2()

    for h in range(harms):
        @pl.when(other(h))
        def _():
            a_copy(h, h, h).wait_send()
        m_copy(h, h).wait_send()
    drain1()
    drain2()


def local(
    tiles,
    harms,
    adjoint,
    objective_grad,
    first_jacobian_blocks,
    second_jacobian_blocks,
    block_column_layout,
    coupling,
    matching,
    intersection,
    modes,
    clocking,
):
    own_hc, group, width = adjoint.shape
    rows, kk = first_jacobian_blocks.shape[:2]
    hc = coupling.shape[0]
    padded = -(-own_hc // 16) * 16
    vmem = pl.BlockSpec(memory_space=pltpu.VMEM)
    smem = pl.BlockSpec(memory_space=pltpu.SMEM)
    hbm = pl.BlockSpec(memory_space=pl.ANY)
    f32, bf16 = jnp.float32, jnp.bfloat16
    dma = pltpu.SemaphoreType.DMA
    second = pl.pallas_call(
        functools.partial(kernel, tiles, harms),
        out_shape=jax.ShapeDtypeStruct((group * own_hc, width), f32),
        in_specs=[vmem, smem, vmem, smem, smem, smem, smem, hbm, hbm],
        out_specs=vmem,
        scratch_shapes=[
            pltpu.VMEM(first_jacobian_blocks.shape, bf16),
            pltpu.VMEM(first_jacobian_blocks.shape, bf16),
            pltpu.VMEM((group, padded, width), f32),
            pltpu.VMEM((harms, rows, padded, width), bf16),
            pltpu.VMEM((harms, rows, padded, width), bf16),
            pltpu.VMEM((rows, hc, width), f32),
            pltpu.VMEM((rows * kk, hc, width), f32),
            pltpu.VMEM((3 * harms, rows, hc, width), f32),
            pltpu.VMEM((3 * harms, rows, hc, width), f32),
            pltpu.VMEM((rows, hc, LANES), f32),
            pltpu.VMEM((harms, rows, hc, LANES), f32),
            pltpu.VMEM((rows, hc, LANES), f32),
            pltpu.VMEM((3 * harms, group * own_hc, width), f32),
            pltpu.VMEM((3 * harms, group * own_hc, width), f32),
            dma((rows * kk,)),
            dma((rows * kk,)),
            dma((harms,)),
            dma((harms,)),
            dma((3 * harms,)),
            dma((3 * harms,)),
            dma((harms,)),
            dma((harms,)),
            dma((3 * harms,)),
            dma((3 * harms,)),
        ],
        compiler_params=pltpu.CompilerParams(
            collective_id=0, has_side_effects=True, vmem_limit_bytes=40 * 1024 * 1024
        ),
    )(
        adjoint,
        block_column_layout,
        coupling,
        matching,
        intersection,
        modes,
        clocking,
        first_jacobian_blocks,
        second_jacobian_blocks,
    )
    return objective_grad - jnp.transpose(second.reshape(group, own_hc, width), (1, 0, 2))


def solution(mesh):
    return jax.shard_map(
        functools.partial(local, mesh.shape["tile"], mesh.shape["harm"]),
        mesh=mesh,
        in_specs=(
            P("harm", "tile", None),
            P("harm", "tile", None),
            P(("tile", "harm"), None, None, None),
            P(("tile", "harm"), None, None, None),
            P("tile", None),
            P(),
            P("tile", None),
            P("tile", None),
            P(),
            P("tile"),
        ),
        out_specs=P("harm", "tile", None),
        check_vma=False,
    )
```

```python
import functools

import jax
import jax.numpy as jnp
from jax import lax
from jax.experimental import pallas as pl
from jax.experimental.pallas import tpu as pltpu
from jax.sharding import PartitionSpec as P

VARS = 5
IF_CELLS = 8
STRIP = VARS * IF_CELLS
LANES = 128
VMEM_BYTES = 62 * 1024 * 1024
MESH = pl.DeviceIdType.MESH


def kernel(
    tiles,
    harms,
    adj_hbm,
    layout_hbm,
    coupling_hbm,
    matching_hbm,
    weights_hbm,
    modes_hbm,
    clocking_hbm,
    first_hbm,
    second_hbm,
    out,
    adj,
    layout,
    coupling,
    matching,
    weights,
    modes,
    clocking,
    first_j,
    second_j,
    pad,
    a_send,
    a_recv,
    full,
    terms,
    send1,
    recv1,
    m_send,
    m_recv,
    swap,
    send2,
    recv2,
    in_sem,
    j1_sem,
    j2_sem,
    a_ssem,
    a_rsem,
    s1_sem,
    r1_sem,
    m_ssem,
    m_rsem,
    s2_sem,
    r2_sem,
):
    my_t = lax.axis_index("tile")
    my_h = lax.axis_index("harm")
    own_hc, group, width = adj.shape
    rows, kk = first_j.shape[0], first_j.shape[1]
    hc = coupling.shape[0]
    half = hc // 2
    base = my_h * rows
    far = lax.rem(my_t + tiles // 2, tiles)
    near = [lax.rem(my_t + tiles - 1, tiles), my_t, lax.rem(my_t + 1, tiles)]

    def block_copies(hbm, vmem, sem):
        return [
            pltpu.make_async_copy(hbm.at[r, k], vmem.at[r, k], sem.at[r * kk + k])
            for r in range(rows)
            for k in range(kk)
        ]

    first_copies = block_copies(first_hbm, first_j, j1_sem)
    second_copies = block_copies(second_hbm, second_j, j2_sem)
    pairs = [
        (adj_hbm, adj),
        (layout_hbm, layout),
        (coupling_hbm, coupling),
        (matching_hbm, matching),
        (weights_hbm, weights),
        (modes_hbm, modes),
        (clocking_hbm, clocking),
    ]
    in_copies = [
        pltpu.make_async_copy(src, dst, in_sem.at[i]) for i, (src, dst) in enumerate(pairs)
    ]
    for copy in in_copies:
        copy.start()
    for copy in first_copies:
        copy.start()

    barrier = pltpu.get_barrier_semaphore()
    for d in (-1, 0, 1):
        for h in range(harms):
            if d == 0:
                @pl.when(h != my_h)
                def _():
                    pl.semaphore_signal(barrier, inc=1, device_id=(my_t, h), device_id_type=MESH)
            else:
                pl.semaphore_signal(barrier, inc=1, device_id=(near[d + 1], h), device_id_type=MESH)
    for h in range(harms):
        pl.semaphore_signal(barrier, inc=1, device_id=(far, h), device_id_type=MESH)

    pad[...] = jnp.zeros_like(pad)
    in_copies[0].wait()
    for h in range(harms):
        for r in range(rows):
            pad[h * rows + r, 0:own_hc, :] = adj[:, h * rows + r, :]
    for h in range(harms):
        for r in range(rows):
            a_send[h, r] = pad[h * rows + r].astype(jnp.bfloat16)

    pl.semaphore_wait(barrier, 4 * harms - 1)

    def a_copy(to, slot, sem):
        return pltpu.make_async_remote_copy(
            src_ref=a_send.at[to],
            dst_ref=a_recv.at[slot],
            send_sem=a_ssem.at[to],
            recv_sem=a_rsem.at[sem],
            device_id=(my_t, to),
            device_id_type=MESH,
        )

    def other(h):
        return h != my_h

    for h in range(harms):
        @pl.when(other(h))
        def _():
            a_copy(h, my_h, my_h).start()

    for copy in second_copies:
        copy.start()

    a_recv[my_h] = a_send[my_h]

    for copy in in_copies[1:]:
        copy.wait()
    row_id = lax.broadcasted_iota(jnp.int32, (hc, LANES), 0)
    lane_id = lax.broadcasted_iota(jnp.int32, (hc, LANES), 1)
    mode = jnp.zeros((hc, LANES), jnp.float32)
    for n in range(half):
        value = modes[n].astype(jnp.float32)
        mode = jnp.where((row_id == n) | (row_id == n + half), value, mode)
    cosines, sines = [], []
    for r in range(rows):
        phi = mode * clocking[base + r]
        inside = lane_id < STRIP
        sine = jnp.sin(phi)
        cosines.append(jnp.where(inside, jnp.cos(phi), 0.0))
        sines.append(jnp.where(inside, jnp.where(row_id < half, -sine, sine), 0.0))

    spot = [[layout[base + r, k] for k in range(kk)] for r in range(rows)]

    def one(r, k, slot):
        return jnp.where(spot[r][k] == slot, 1.0, 0.0).astype(jnp.float32)

    def fold(slot):
        total = None
        for r in range(rows):
            for k in range(kk):
                term = one(r, k, slot) * terms[r * kk + k]
                total = term if total is None else total + term
        return total

    for copy in first_copies:
        copy.wait()
    for h in range(harms):
        @pl.when(other(h))
        def _():
            a_copy(h, h, h).wait_recv()
    for r in range(rows):
        for h in range(harms):
            full[r, h * own_hc : (h + 1) * own_hc, :] = a_recv[h, r].astype(jnp.float32)[0:own_hc]

    def products(vectors, blocks):
        for r in range(rows):
            for k in range(kk):
                terms[r * kk + k] = jnp.dot(
                    vectors[r], blocks[r, k], preferred_element_type=jnp.float32
                )

    def exchange(send, recv, ssem, rsem):
        def copy(d, to, slot):
            return pltpu.make_async_remote_copy(
                src_ref=send.at[(d + 1) * harms + to],
                dst_ref=recv.at[slot],
                send_sem=ssem.at[(d + 1) * harms + to],
                recv_sem=rsem.at[slot],
                device_id=(near[d + 1], to),
                device_id_type=MESH,
            )

        def start(d, to):
            if d == 0:
                @pl.when(other(to))
                def _():
                    copy(d, to, harms + my_h).start()
            else:
                copy(d, to, (d + 1) * harms + my_h).start()

        def finish(d, h):
            if d == 0:
                @pl.when(other(h))
                def _():
                    copy(d, h, harms + h).wait_recv()
            else:
                copy(d, h, (d + 1) * harms + h).wait_recv()

        def drain():
            for d in (-1, 0, 1):
                for h in range(harms):
                    if d == 0:
                        @pl.when(other(h))
                        def _():
                            copy(d, h, harms + h).wait_send()
                    else:
                        copy(d, h, (d + 1) * harms + h).wait_send()

        def collect():
            total = send[harms + my_h]
            for d in (-1, 1, 0):
                for h in range(harms):
                    finish(d, h)
                if d == 0:
                    for j in range(1, harms):
                        total = total + recv[harms + lax.rem(my_h + j, harms)]
                else:
                    for h in range(harms):
                        total = total + recv[(d + 1) * harms + h]
            return total

        return start, collect, drain

    start1, collect1, drain1 = exchange(send1, recv1, s1_sem, r1_sem)
    start2, collect2, drain2 = exchange(send2, recv2, s2_sem, r2_sem)

    products([full[r].astype(jnp.bfloat16) for r in range(rows)], first_j)
    for d in (-1, 1, 0):
        for h in range(harms):
            for r in range(rows):
                send1[(d + 1) * harms + h, r] = fold((d + 1) * group + h * rows + r)
            start1(d, h)
    first = collect1()

    m_send[...] = first[:, :, 0:LANES]

    def m_copy(to, slot):
        return pltpu.make_async_remote_copy(
            src_ref=m_send,
            dst_ref=m_recv.at[slot],
            send_sem=m_ssem.at[to],
            recv_sem=m_rsem.at[slot],
            device_id=(far, to),
            device_id_type=MESH,
        )

    for h in range(harms):
        m_copy(h, my_h).start()
    plain = []
    for r in range(rows):
        plain.append(
            first[r]
            + jnp.dot(
                coupling[...],
                first[r],
                precision=lax.Precision.HIGHEST,
                preferred_element_type=jnp.float32,
            )
        )
    for copy in second_copies:
        copy.wait()
    for r in range(rows):
        tail = plain[r][:, LANES:].astype(jnp.bfloat16)
        for k in range(kk):
            terms[r * kk + k] = jnp.dot(
                tail, second_j[r, k, LANES:, :], preferred_element_type=jnp.float32
            )
    for h in range(harms):
        m_copy(h, h).wait_recv()
    for r in range(rows):
        mortar = jnp.zeros((hc, LANES), jnp.float32)
        for h in range(harms):
            for q in range(rows):
                place = h * rows + q
                weight = jnp.where(matching[0, base + r] == place, weights[0, base + r], 0.0)
                weight = weight + jnp.where(matching[1, base + r] == place, weights[1, base + r], 0.0)
                mortar = mortar + weight * m_recv[h, q]
        swap[r, 0:half, :] = mortar[half:]
        swap[r, half:, :] = mortar[0:half]
        rotated = cosines[r] * mortar + sines[r] * swap[r]
        head = (plain[r][:, 0:LANES] + rotated).astype(jnp.bfloat16)
        for k in range(kk):
            terms[r * kk + k] += jnp.dot(
                head, second_j[r, k, 0:LANES, :], preferred_element_type=jnp.float32
            )

    for d in (-1, 1, 0):
        for s in range(group):
            value = fold((d + 1) * group + s)
            for h in range(harms):
                send2[(d + 1) * harms + h, s * own_hc : (s + 1) * own_hc, :] = value[
                    h * own_hc : (h + 1) * own_hc
                ]
        for h in range(harms):
            start2(d, h)
    out[...] = collect2()

    for h in range(harms):
        @pl.when(other(h))
        def _():
            a_copy(h, h, h).wait_send()
        m_copy(h, h).wait_send()
    drain1()
    drain2()


def local(
    tiles,
    harms,
    adjoint,
    objective_grad,
    first_jacobian_blocks,
    second_jacobian_blocks,
    block_column_layout,
    coupling,
    matching,
    intersection,
    modes,
    clocking,
):
    own_hc, group, width = adjoint.shape
    rows, kk = first_jacobian_blocks.shape[:2]
    hc = coupling.shape[0]
    padded = -(-own_hc // 16) * 16
    vmem = pl.BlockSpec(memory_space=pltpu.VMEM)
    hbm = pl.BlockSpec(memory_space=pl.ANY)
    f32, bf16 = jnp.float32, jnp.bfloat16
    dma = pltpu.SemaphoreType.DMA
    second = pl.pallas_call(
        functools.partial(kernel, tiles, harms),
        out_shape=jax.ShapeDtypeStruct((group * own_hc, width), f32),
        in_specs=[hbm] * 9,
        out_specs=vmem,
        scratch_shapes=[
            pltpu.VMEM(adjoint.shape, f32),
            pltpu.SMEM(block_column_layout.shape, jnp.int32),
            pltpu.VMEM(coupling.shape, f32),
            pltpu.SMEM(matching.shape[::-1], jnp.int32),
            pltpu.SMEM(intersection.shape[::-1], f32),
            pltpu.SMEM(modes.shape, jnp.int32),
            pltpu.SMEM(clocking.shape, f32),
            pltpu.VMEM(first_jacobian_blocks.shape, bf16),
            pltpu.VMEM(first_jacobian_blocks.shape, bf16),
            pltpu.VMEM((group, padded, width), f32),
            pltpu.VMEM((harms, rows, padded, width), bf16),
            pltpu.VMEM((harms, rows, padded, width), bf16),
            pltpu.VMEM((rows, hc, width), f32),
            pltpu.VMEM((rows * kk, hc, width), f32),
            pltpu.VMEM((3 * harms, rows, hc, width), f32),
            pltpu.VMEM((3 * harms, rows, hc, width), f32),
            pltpu.VMEM((rows, hc, LANES), f32),
            pltpu.VMEM((harms, rows, hc, LANES), f32),
            pltpu.VMEM((rows, hc, LANES), f32),
            pltpu.VMEM((3 * harms, group * own_hc, width), f32),
            pltpu.VMEM((3 * harms, group * own_hc, width), f32),
            dma((7,)),
            dma((rows * kk,)),
            dma((rows * kk,)),
            dma((harms,)),
            dma((harms,)),
            dma((3 * harms,)),
            dma((3 * harms,)),
            dma((harms,)),
            dma((harms,)),
            dma((3 * harms,)),
            dma((3 * harms,)),
        ],
        compiler_params=pltpu.CompilerParams(
            collective_id=0, has_side_effects=True, vmem_limit_bytes=VMEM_BYTES
        ),
    )(
        adjoint,
        block_column_layout,
        coupling,
        matching.T,
        intersection.T,
        modes,
        clocking,
        first_jacobian_blocks,
        second_jacobian_blocks,
    )
    return objective_grad - jnp.transpose(second.reshape(group, own_hc, width), (1, 0, 2))


def solution(mesh):
    return jax.shard_map(
        functools.partial(local, mesh.shape["tile"], mesh.shape["harm"]),
        mesh=mesh,
        in_specs=(
            P("harm", "tile", None),
            P("harm", "tile", None),
            P(("tile", "harm"), None, None, None),
            P(("tile", "harm"), None, None, None),
            P("tile", None),
            P(),
            P("tile", None),
            P("tile", None),
            P(),
            P("tile"),
        ),
        out_specs=P("harm", "tile", None),
        check_vma=False,
    )
```

```python
import functools

import jax
import jax.numpy as jnp
from jax import lax
from jax.experimental import pallas as pl
from jax.experimental.pallas import tpu as pltpu
from jax.sharding import PartitionSpec as P

VARS = 5
IF_CELLS = 8
STRIP = VARS * IF_CELLS
LANES = 128
VMEM_BYTES = 62 * 1024 * 1024
MESH = pl.DeviceIdType.MESH


def kernel(
    tiles,
    harms,
    adj_hbm,
    layout_hbm,
    coupling_hbm,
    matching_hbm,
    weights_hbm,
    modes_hbm,
    clocking_hbm,
    grad_hbm,
    first_hbm,
    second_hbm,
    out,
    adj,
    layout,
    coupling,
    matching,
    weights,
    modes,
    clocking,
    grad,
    first_j,
    second_j,
    pad,
    a_send,
    a_recv,
    full,
    terms,
    send1,
    recv1,
    m_send,
    m_recv,
    swap,
    stage,
    send2,
    recv2,
    in_sem,
    j1_sem,
    j2_sem,
    a_ssem,
    a_rsem,
    s1_sem,
    r1_sem,
    m_ssem,
    m_rsem,
    s2_sem,
    r2_sem,
):
    my_t = lax.axis_index("tile")
    my_h = lax.axis_index("harm")
    own_hc, group, width = adj.shape
    rows, kk = first_j.shape[0], first_j.shape[1]
    hc = coupling.shape[0]
    half = hc // 2
    base = my_h * rows
    far = lax.rem(my_t + tiles // 2, tiles)
    near = [lax.rem(my_t + tiles - 1, tiles), my_t, lax.rem(my_t + 1, tiles)]

    barrier = pltpu.get_barrier_semaphore()
    for d in (-1, 0, 1):
        for h in range(harms):
            if d == 0:
                @pl.when(h != my_h)
                def _():
                    pl.semaphore_signal(barrier, inc=1, device_id=(my_t, h), device_id_type=MESH)
            else:
                pl.semaphore_signal(barrier, inc=1, device_id=(near[d + 1], h), device_id_type=MESH)
    for h in range(harms):
        pl.semaphore_signal(barrier, inc=1, device_id=(far, h), device_id_type=MESH)

    def block_copies(hbm, vmem, sem):
        return [
            pltpu.make_async_copy(hbm.at[r, k], vmem.at[r, k], sem.at[r * kk + k])
            for r in range(rows)
            for k in range(kk)
        ]

    first_copies = block_copies(first_hbm, first_j, j1_sem)
    second_copies = block_copies(second_hbm, second_j, j2_sem)
    pairs = [
        (adj_hbm, adj),
        (layout_hbm, layout),
        (coupling_hbm, coupling),
        (matching_hbm, matching),
        (weights_hbm, weights),
        (modes_hbm, modes),
        (clocking_hbm, clocking),
        (grad_hbm, grad),
    ]
    in_copies = [
        pltpu.make_async_copy(src, dst, in_sem.at[i]) for i, (src, dst) in enumerate(pairs)
    ]
    for copy in in_copies:
        copy.start()
    for copy in first_copies:
        copy.start()

    pad[...] = jnp.zeros_like(pad)
    in_copies[0].wait()
    for h in range(harms):
        for r in range(rows):
            pad[h * rows + r, 0:own_hc, :] = adj[:, h * rows + r, :]
    for h in range(harms):
        for r in range(rows):
            a_send[h, r] = pad[h * rows + r].astype(jnp.bfloat16)

    pl.semaphore_wait(barrier, 4 * harms - 1)

    def a_copy(to, slot, sem):
        return pltpu.make_async_remote_copy(
            src_ref=a_send.at[to],
            dst_ref=a_recv.at[slot],
            send_sem=a_ssem.at[to],
            recv_sem=a_rsem.at[sem],
            device_id=(my_t, to),
            device_id_type=MESH,
        )

    def other(h):
        return h != my_h

    for h in range(harms):
        @pl.when(other(h))
        def _():
            a_copy(h, my_h, my_h).start()

    for copy in second_copies:
        copy.start()

    a_recv[my_h] = a_send[my_h]

    for copy in in_copies[1:]:
        copy.wait()
    row_id = lax.broadcasted_iota(jnp.int32, (hc, LANES), 0)
    lane_id = lax.broadcasted_iota(jnp.int32, (hc, LANES), 1)
    mode = jnp.zeros((hc, LANES), jnp.float32)
    for n in range(half):
        value = modes[n].astype(jnp.float32)
        mode = jnp.where((row_id == n) | (row_id == n + half), value, mode)
    cosines, sines = [], []
    for r in range(rows):
        phi = mode * clocking[base + r]
        inside = lane_id < STRIP
        sine = jnp.sin(phi)
        cosines.append(jnp.where(inside, jnp.cos(phi), 0.0))
        sines.append(jnp.where(inside, jnp.where(row_id < half, -sine, sine), 0.0))

    spot = [[layout[base + r, k] for k in range(kk)] for r in range(rows)]

    def one(r, k, slot):
        return jnp.where(spot[r][k] == slot, 1.0, 0.0).astype(jnp.float32)

    def fold(slot):
        total = None
        for r in range(rows):
            for k in range(kk):
                term = one(r, k, slot) * terms[r * kk + k]
                total = term if total is None else total + term
        return total

    for copy in first_copies:
        copy.wait()
    for h in range(harms):
        @pl.when(other(h))
        def _():
            a_copy(h, h, h).wait_recv()
    for r in range(rows):
        for h in range(harms):
            full[r, h * own_hc : (h + 1) * own_hc, :] = a_recv[h, r].astype(jnp.float32)[0:own_hc]

    def products(vectors, blocks):
        for r in range(rows):
            for k in range(kk):
                terms[r * kk + k] = jnp.dot(
                    vectors[r], blocks[r, k], preferred_element_type=jnp.float32
                )

    def exchange(send, recv, ssem, rsem):
        def copy(d, to, slot):
            return pltpu.make_async_remote_copy(
                src_ref=send.at[(d + 1) * harms + to],
                dst_ref=recv.at[slot],
                send_sem=ssem.at[(d + 1) * harms + to],
                recv_sem=rsem.at[slot],
                device_id=(near[d + 1], to),
                device_id_type=MESH,
            )

        def start(d, to):
            if d == 0:
                @pl.when(other(to))
                def _():
                    copy(d, to, harms + my_h).start()
            else:
                copy(d, to, (d + 1) * harms + my_h).start()

        def finish(d, h):
            if d == 0:
                @pl.when(other(h))
                def _():
                    copy(d, h, harms + h).wait_recv()
            else:
                copy(d, h, (d + 1) * harms + h).wait_recv()

        def drain():
            for d in (-1, 0, 1):
                for h in range(harms):
                    if d == 0:
                        @pl.when(other(h))
                        def _():
                            copy(d, h, harms + h).wait_send()
                    else:
                        copy(d, h, (d + 1) * harms + h).wait_send()

        def collect(total):
            for d in (-1, 1, 0):
                for h in range(harms):
                    finish(d, h)
                if d == 0:
                    for j in range(1, harms):
                        slot = harms + lax.rem(my_h + j, harms)
                        total = total + recv[slot].astype(jnp.float32)
                else:
                    for h in range(harms):
                        total = total + recv[(d + 1) * harms + h].astype(jnp.float32)
            return total

        return start, collect, drain

    start1, collect1, drain1 = exchange(send1, recv1, s1_sem, r1_sem)
    start2, collect2, drain2 = exchange(send2, recv2, s2_sem, r2_sem)

    products([full[r].astype(jnp.bfloat16) for r in range(rows)], first_j)
    for d in (-1, 1, 0):
        for h in range(harms):
            for r in range(rows):
                send1[(d + 1) * harms + h, r] = fold((d + 1) * group + h * rows + r)
            start1(d, h)
    first = collect1(send1[harms + my_h])

    gap = LANES // rows
    assert gap >= STRIP
    packed = first[0][:, 0:LANES]
    for r in range(1, rows):
        moved = pltpu.roll(first[r][:, 0:LANES], r * gap, 1)
        packed = jnp.where(lane_id >= r * gap, moved, packed)
    m_send[...] = packed

    def m_copy(to, slot):
        return pltpu.make_async_remote_copy(
            src_ref=m_send,
            dst_ref=m_recv.at[slot],
            send_sem=m_ssem.at[to],
            recv_sem=m_rsem.at[slot],
            device_id=(far, to),
            device_id_type=MESH,
        )

    for h in range(harms):
        m_copy(h, my_h).start()
    plain = []
    for r in range(rows):
        plain.append(
            first[r]
            + jnp.dot(
                coupling[...],
                first[r],
                precision=lax.Precision.HIGHEST,
                preferred_element_type=jnp.float32,
            )
        )
    for copy in second_copies:
        copy.wait()
    for r in range(rows):
        tail = plain[r][:, LANES:].astype(jnp.bfloat16)
        for k in range(kk):
            terms[r * kk + k] = jnp.dot(
                tail, second_j[r, k, LANES:, :], preferred_element_type=jnp.float32
            )
    for h in range(harms):
        m_copy(h, h).wait_recv()
    for r in range(rows):
        mortar = jnp.zeros((hc, LANES), jnp.float32)
        for q in range(rows):
            part = jnp.zeros((hc, LANES), jnp.float32)
            for h in range(harms):
                place = h * rows + q
                weight = jnp.where(matching[0, base + r] == place, weights[0, base + r], 0.0)
                weight = weight + jnp.where(matching[1, base + r] == place, weights[1, base + r], 0.0)
                part = part + weight * m_recv[h]
            mortar = mortar + (part if q == 0 else pltpu.roll(part, LANES - q * gap, 1))
        swap[r, 0:half, :] = mortar[half:]
        swap[r, half:, :] = mortar[0:half]
        rotated = cosines[r] * mortar + sines[r] * swap[r]
        head = (plain[r][:, 0:LANES] + rotated).astype(jnp.bfloat16)
        for k in range(kk):
            terms[r * kk + k] += jnp.dot(
                head, second_j[r, k, 0:LANES, :], preferred_element_type=jnp.float32
            )

    for d in (-1, 1, 0):
        for s in range(group):
            value = fold((d + 1) * group + s)
            for h in range(harms):
                stage[h, s * own_hc : (s + 1) * own_hc, :] = value[
                    h * own_hc : (h + 1) * own_hc
                ]
        for h in range(harms):
            send2[(d + 1) * harms + h] = stage[h].astype(jnp.bfloat16)
            start2(d, h)
    second = collect2(stage[my_h])
    for s in range(group):
        out[:, s, :] = grad[:, s, :] - second[s * own_hc : (s + 1) * own_hc]

    for h in range(harms):
        @pl.when(other(h))
        def _():
            a_copy(h, h, h).wait_send()
        m_copy(h, h).wait_send()
    drain1()
    drain2()


def local(
    tiles,
    harms,
    adjoint,
    objective_grad,
    first_jacobian_blocks,
    second_jacobian_blocks,
    block_column_layout,
    coupling,
    matching,
    intersection,
    modes,
    clocking,
):
    own_hc, group, width = adjoint.shape
    rows, kk = first_jacobian_blocks.shape[:2]
    hc = coupling.shape[0]
    padded = -(-own_hc // 16) * 16
    vmem = pl.BlockSpec(memory_space=pltpu.VMEM)
    hbm = pl.BlockSpec(memory_space=pl.ANY)
    f32, bf16 = jnp.float32, jnp.bfloat16
    dma = pltpu.SemaphoreType.DMA
    return pl.pallas_call(
        functools.partial(kernel, tiles, harms),
        out_shape=jax.ShapeDtypeStruct(objective_grad.shape, f32),
        in_specs=[hbm] * 10,
        out_specs=vmem,
        scratch_shapes=[
            pltpu.VMEM(adjoint.shape, f32),
            pltpu.SMEM(block_column_layout.shape, jnp.int32),
            pltpu.VMEM(coupling.shape, f32),
            pltpu.SMEM(matching.shape[::-1], jnp.int32),
            pltpu.SMEM(intersection.shape[::-1], f32),
            pltpu.SMEM(modes.shape, jnp.int32),
            pltpu.SMEM(clocking.shape, f32),
            pltpu.VMEM(objective_grad.shape, f32),
            pltpu.VMEM(first_jacobian_blocks.shape, bf16),
            pltpu.VMEM(first_jacobian_blocks.shape, bf16),
            pltpu.VMEM((group, padded, width), f32),
            pltpu.VMEM((harms, rows, padded, width), bf16),
            pltpu.VMEM((harms, rows, padded, width), bf16),
            pltpu.VMEM((rows, hc, width), f32),
            pltpu.VMEM((rows * kk, hc, width), f32),
            pltpu.VMEM((3 * harms, rows, hc, width), f32),
            pltpu.VMEM((3 * harms, rows, hc, width), f32),
            pltpu.VMEM((hc, LANES), f32),
            pltpu.VMEM((harms, hc, LANES), f32),
            pltpu.VMEM((rows, hc, LANES), f32),
            pltpu.VMEM((harms, group * own_hc, width), f32),
            pltpu.VMEM((3 * harms, group * own_hc, width), bf16),
            pltpu.VMEM((3 * harms, group * own_hc, width), bf16),
            dma((8,)),
            dma((rows * kk,)),
            dma((rows * kk,)),
            dma((harms,)),
            dma((harms,)),
            dma((3 * harms,)),
            dma((3 * harms,)),
            dma((harms,)),
            dma((harms,)),
            dma((3 * harms,)),
            dma((3 * harms,)),
        ],
        compiler_params=pltpu.CompilerParams(
            collective_id=0, has_side_effects=True, vmem_limit_bytes=VMEM_BYTES
        ),
    )(
        adjoint,
        block_column_layout,
        coupling,
        matching.T,
        intersection.T,
        modes,
        clocking,
        objective_grad,
        first_jacobian_blocks,
        second_jacobian_blocks,
    )


def solution(mesh):
    return jax.shard_map(
        functools.partial(local, mesh.shape["tile"], mesh.shape["harm"]),
        mesh=mesh,
        in_specs=(
            P("harm", "tile", None),
            P("harm", "tile", None),
            P(("tile", "harm"), None, None, None),
            P(("tile", "harm"), None, None, None),
            P("tile", None),
            P(),
            P("tile", None),
            P("tile", None),
            P(),
            P("tile"),
        ),
        out_specs=P("harm", "tile", None),
        check_vma=False,
    )
```

```python
import functools

import jax
import jax.numpy as jnp
from jax import lax
from jax.experimental import pallas as pl
from jax.experimental.pallas import tpu as pltpu
from jax.sharding import PartitionSpec as P

VARS = 5
IF_CELLS = 8
STRIP = VARS * IF_CELLS
LANES = 128
VMEM_BYTES = 62 * 1024 * 1024
MESH = pl.DeviceIdType.MESH


def kernel(
    tiles,
    harms,
    adj_hbm,
    layout_hbm,
    coupling_hbm,
    matching_hbm,
    weights_hbm,
    modes_hbm,
    clocking_hbm,
    first_hbm,
    second_hbm,
    out,
    adj,
    layout,
    coupling,
    matching,
    weights,
    modes,
    clocking,
    first_j,
    second_j,
    pad,
    a_send,
    a_recv,
    full,
    terms,
    send1a,
    recv1a,
    send1b,
    recv1b,
    m_send,
    m_recv,
    swap,
    stage,
    send2,
    recv2,
    in_sem,
    j1_sem,
    j2_sem,
    a_ssem,
    a_rsem,
    s1a_sem,
    r1a_sem,
    s1b_sem,
    r1b_sem,
    m_ssem,
    m_rsem,
    s2_sem,
    r2_sem,
):
    my_t = lax.axis_index("tile")
    my_h = lax.axis_index("harm")
    own_hc, group, width = adj.shape
    rows, kk = first_j.shape[0], first_j.shape[1]
    hc = coupling.shape[0]
    half = hc // 2
    base = my_h * rows
    far = lax.rem(my_t + tiles // 2, tiles)
    near = [lax.rem(my_t + tiles - 1, tiles), my_t, lax.rem(my_t + 1, tiles)]

    barrier = pltpu.get_barrier_semaphore()
    for d in (-1, 0, 1):
        for h in range(harms):
            if d == 0:
                @pl.when(h != my_h)
                def _():
                    pl.semaphore_signal(barrier, inc=1, device_id=(my_t, h), device_id_type=MESH)
            else:
                pl.semaphore_signal(barrier, inc=1, device_id=(near[d + 1], h), device_id_type=MESH)
    for h in range(harms):
        pl.semaphore_signal(barrier, inc=1, device_id=(far, h), device_id_type=MESH)

    def block_copies(hbm, vmem, sem):
        return [
            pltpu.make_async_copy(hbm.at[r, k], vmem.at[r, k], sem.at[r * kk + k])
            for r in range(rows)
            for k in range(kk)
        ]

    first_copies = block_copies(first_hbm, first_j, j1_sem)
    second_copies = block_copies(second_hbm, second_j, j2_sem)
    pairs = [
        (adj_hbm, adj),
        (layout_hbm, layout),
        (coupling_hbm, coupling),
        (matching_hbm, matching),
        (weights_hbm, weights),
        (modes_hbm, modes),
        (clocking_hbm, clocking),
    ]
    in_copies = [
        pltpu.make_async_copy(src, dst, in_sem.at[i]) for i, (src, dst) in enumerate(pairs)
    ]
    for copy in in_copies:
        copy.start()
    for copy in first_copies:
        copy.start()

    pad[...] = jnp.zeros_like(pad)
    in_copies[0].wait()
    for h in range(harms):
        for r in range(rows):
            pad[h * rows + r, 0:own_hc, :] = adj[:, h * rows + r, :]
    for h in range(harms):
        for r in range(rows):
            a_send[h, r] = pad[h * rows + r].astype(jnp.bfloat16)

    pl.semaphore_wait(barrier, 4 * harms - 1)

    def a_copy(to, slot, sem):
        return pltpu.make_async_remote_copy(
            src_ref=a_send.at[to],
            dst_ref=a_recv.at[slot],
            send_sem=a_ssem.at[to],
            recv_sem=a_rsem.at[sem],
            device_id=(my_t, to),
            device_id_type=MESH,
        )

    def other(h):
        return h != my_h

    for h in range(harms):
        @pl.when(other(h))
        def _():
            a_copy(h, my_h, my_h).start()

    for copy in second_copies:
        copy.start()

    a_recv[my_h] = a_send[my_h]

    for copy in in_copies[1:]:
        copy.wait()
    row_id = lax.broadcasted_iota(jnp.int32, (hc, LANES), 0)
    lane_id = lax.broadcasted_iota(jnp.int32, (hc, LANES), 1)
    mode = jnp.zeros((hc, LANES), jnp.float32)
    for n in range(half):
        value = modes[n].astype(jnp.float32)
        mode = jnp.where((row_id == n) | (row_id == n + half), value, mode)
    cosines, sines = [], []
    for r in range(rows):
        phi = mode * clocking[base + r]
        inside = lane_id < STRIP
        sine = jnp.sin(phi)
        cosines.append(jnp.where(inside, jnp.cos(phi), 0.0))
        sines.append(jnp.where(inside, jnp.where(row_id < half, -sine, sine), 0.0))

    spot = [[layout[base + r, k] for k in range(kk)] for r in range(rows)]

    def one(r, k, slot):
        return jnp.where(spot[r][k] == slot, 1.0, 0.0).astype(jnp.float32)

    def fold(slot, low, high):
        total = None
        for r in range(rows):
            for k in range(kk):
                term = one(r, k, slot) * terms[r * kk + k, :, low:high]
                total = term if total is None else total + term
        return total

    for copy in first_copies:
        copy.wait()
    for h in range(harms):
        @pl.when(other(h))
        def _():
            a_copy(h, h, h).wait_recv()
    for r in range(rows):
        for h in range(harms):
            full[r, h * own_hc : (h + 1) * own_hc, :] = a_recv[h, r].astype(jnp.float32)[0:own_hc]

    def exchange(send, recv, ssem, rsem):
        def copy(d, to, slot):
            return pltpu.make_async_remote_copy(
                src_ref=send.at[(d + 1) * harms + to],
                dst_ref=recv.at[slot],
                send_sem=ssem.at[(d + 1) * harms + to],
                recv_sem=rsem.at[slot],
                device_id=(near[d + 1], to),
                device_id_type=MESH,
            )

        def start(d, to):
            if d == 0:
                @pl.when(other(to))
                def _():
                    copy(d, to, harms + my_h).start()
            else:
                copy(d, to, (d + 1) * harms + my_h).start()

        def finish(d, h):
            if d == 0:
                @pl.when(other(h))
                def _():
                    copy(d, h, harms + h).wait_recv()
            else:
                copy(d, h, (d + 1) * harms + h).wait_recv()

        def drain():
            for d in (-1, 0, 1):
                for h in range(harms):
                    if d == 0:
                        @pl.when(other(h))
                        def _():
                            copy(d, h, harms + h).wait_send()
                    else:
                        copy(d, h, (d + 1) * harms + h).wait_send()

        def collect(total):
            for d in (-1, 1, 0):
                for h in range(harms):
                    finish(d, h)
                if d == 0:
                    for j in range(1, harms):
                        slot = harms + lax.rem(my_h + j, harms)
                        total = total + recv[slot].astype(jnp.float32)
                else:
                    for h in range(harms):
                        total = total + recv[(d + 1) * harms + h].astype(jnp.float32)
            return total

        return start, collect, drain

    start1a, collect1a, drain1a = exchange(send1a, recv1a, s1a_sem, r1a_sem)
    start1b, collect1b, drain1b = exchange(send1b, recv1b, s1b_sem, r1b_sem)
    start2, collect2, drain2 = exchange(send2, recv2, s2_sem, r2_sem)

    vectors = [full[r].astype(jnp.bfloat16) for r in range(rows)]
    for low, high, send, start in ((0, LANES, send1a, start1a), (LANES, width, send1b, start1b)):
        for r in range(rows):
            for k in range(kk):
                terms[r * kk + k, :, low:high] = jnp.dot(
                    vectors[r],
                    first_j[r, k, :, low:high],
                    preferred_element_type=jnp.float32,
                )
        for d in (-1, 1, 0):
            for h in range(harms):
                for r in range(rows):
                    slot = (d + 1) * group + h * rows + r
                    send[(d + 1) * harms + h, r] = fold(slot, low, high)
                start(d, h)
    first_head = collect1a(send1a[harms + my_h])

    gap = LANES // rows
    assert gap >= STRIP
    packed = first_head[0]
    for r in range(1, rows):
        moved = pltpu.roll(first_head[r], r * gap, 1)
        packed = jnp.where(lane_id >= r * gap, moved, packed)
    m_send[...] = packed

    def m_copy(to, slot):
        return pltpu.make_async_remote_copy(
            src_ref=m_send,
            dst_ref=m_recv.at[slot],
            send_sem=m_ssem.at[to],
            recv_sem=m_rsem.at[slot],
            device_id=(far, to),
            device_id_type=MESH,
        )

    for h in range(harms):
        m_copy(h, my_h).start()

    def mix(part):
        mixed = jnp.dot(
            coupling[...],
            part,
            precision=lax.Precision.HIGHEST,
            preferred_element_type=jnp.float32,
        )
        return part + mixed

    plain_head = [mix(first_head[r]) for r in range(rows)]
    first_tail = collect1b(send1b[harms + my_h])
    for copy in second_copies:
        copy.wait()
    for r in range(rows):
        tail = mix(first_tail[r]).astype(jnp.bfloat16)
        for k in range(kk):
            terms[r * kk + k] = jnp.dot(
                tail, second_j[r, k, LANES:, :], preferred_element_type=jnp.float32
            )
    for h in range(harms):
        m_copy(h, h).wait_recv()
    for r in range(rows):
        mortar = jnp.zeros((hc, LANES), jnp.float32)
        for q in range(rows):
            part = jnp.zeros((hc, LANES), jnp.float32)
            for h in range(harms):
                place = h * rows + q
                weight = jnp.where(matching[0, base + r] == place, weights[0, base + r], 0.0)
                weight = weight + jnp.where(matching[1, base + r] == place, weights[1, base + r], 0.0)
                part = part + weight * m_recv[h]
            mortar = mortar + (part if q == 0 else pltpu.roll(part, LANES - q * gap, 1))
        swap[r, 0:half, :] = mortar[half:]
        swap[r, half:, :] = mortar[0:half]
        rotated = cosines[r] * mortar + sines[r] * swap[r]
        head = (plain_head[r] + rotated).astype(jnp.bfloat16)
        for k in range(kk):
            terms[r * kk + k] += jnp.dot(
                head, second_j[r, k, 0:LANES, :], preferred_element_type=jnp.float32
            )

    for d in (-1, 1, 0):
        for s in range(group):
            value = fold((d + 1) * group + s, 0, width)
            for h in range(harms):
                stage[h, s * own_hc : (s + 1) * own_hc, :] = value[
                    h * own_hc : (h + 1) * own_hc
                ]
        for h in range(harms):
            send2[(d + 1) * harms + h] = stage[h].astype(jnp.bfloat16)
            start2(d, h)
    second = collect2(stage[my_h])
    for s in range(group):
        out[:, s, :] = second[s * own_hc : (s + 1) * own_hc]

    for h in range(harms):
        @pl.when(other(h))
        def _():
            a_copy(h, h, h).wait_send()
        m_copy(h, h).wait_send()
    drain1a()
    drain1b()
    drain2()


def local(
    tiles,
    harms,
    adjoint,
    objective_grad,
    first_jacobian_blocks,
    second_jacobian_blocks,
    block_column_layout,
    coupling,
    matching,
    intersection,
    modes,
    clocking,
):
    own_hc, group, width = adjoint.shape
    rows, kk = first_jacobian_blocks.shape[:2]
    hc = coupling.shape[0]
    padded = -(-own_hc // 16) * 16
    vmem = pl.BlockSpec(memory_space=pltpu.VMEM)
    hbm = pl.BlockSpec(memory_space=pl.ANY)
    f32, bf16 = jnp.float32, jnp.bfloat16
    dma = pltpu.SemaphoreType.DMA
    second = pl.pallas_call(
        functools.partial(kernel, tiles, harms),
        out_shape=jax.ShapeDtypeStruct(objective_grad.shape, f32),
        in_specs=[hbm] * 9,
        out_specs=vmem,
        scratch_shapes=[
            pltpu.VMEM(adjoint.shape, f32),
            pltpu.SMEM(block_column_layout.shape, jnp.int32),
            pltpu.VMEM(coupling.shape, f32),
            pltpu.SMEM(matching.shape[::-1], jnp.int32),
            pltpu.SMEM(intersection.shape[::-1], f32),
            pltpu.SMEM(modes.shape, jnp.int32),
            pltpu.SMEM(clocking.shape, f32),
            pltpu.VMEM(first_jacobian_blocks.shape, bf16),
            pltpu.VMEM(first_jacobian_blocks.shape, bf16),
            pltpu.VMEM((group, padded, width), f32),
            pltpu.VMEM((harms, rows, padded, width), bf16),
            pltpu.VMEM((harms, rows, padded, width), bf16),
            pltpu.VMEM((rows, hc, width), f32),
            pltpu.VMEM((rows * kk, hc, width), f32),
            pltpu.VMEM((3 * harms, rows, hc, LANES), f32),
            pltpu.VMEM((3 * harms, rows, hc, LANES), f32),
            pltpu.VMEM((3 * harms, rows, hc, width - LANES), f32),
            pltpu.VMEM((3 * harms, rows, hc, width - LANES), f32),
            pltpu.VMEM((hc, LANES), f32),
            pltpu.VMEM((harms, hc, LANES), f32),
            pltpu.VMEM((rows, hc, LANES), f32),
            pltpu.VMEM((harms, group * own_hc, width), f32),
            pltpu.VMEM((3 * harms, group * own_hc, width), bf16),
            pltpu.VMEM((3 * harms, group * own_hc, width), bf16),
            dma((7,)),
            dma((rows * kk,)),
            dma((rows * kk,)),
            dma((harms,)),
            dma((harms,)),
            dma((3 * harms,)),
            dma((3 * harms,)),
            dma((3 * harms,)),
            dma((3 * harms,)),
            dma((harms,)),
            dma((harms,)),
            dma((3 * harms,)),
            dma((3 * harms,)),
        ],
        compiler_params=pltpu.CompilerParams(
            collective_id=0, has_side_effects=True, vmem_limit_bytes=VMEM_BYTES
        ),
    )(
        adjoint,
        block_column_layout,
        coupling,
        matching.T,
        intersection.T,
        modes,
        clocking,
        first_jacobian_blocks,
        second_jacobian_blocks,
    )
    return objective_grad - second


def solution(mesh):
    return jax.shard_map(
        functools.partial(local, mesh.shape["tile"], mesh.shape["harm"]),
        mesh=mesh,
        in_specs=(
            P("harm", "tile", None),
            P("harm", "tile", None),
            P(("tile", "harm"), None, None, None),
            P(("tile", "harm"), None, None, None),
            P("tile", None),
            P(),
            P("tile", None),
            P("tile", None),
            P(),
            P("tile"),
        ),
        out_specs=P("harm", "tile", None),
        check_vma=False,
    )
```

```python
import functools

import jax
import jax.numpy as jnp
from jax import lax
from jax.experimental import pallas as pl
from jax.experimental.pallas import tpu as pltpu
from jax.sharding import PartitionSpec as P

VARS = 5
IF_CELLS = 8
STRIP = VARS * IF_CELLS
LANES = 128
VMEM_BYTES = 62 * 1024 * 1024
MESH = pl.DeviceIdType.MESH


def kernel(
    tiles,
    harms,
    adj_hbm,
    layout_hbm,
    coupling_hbm,
    matching_hbm,
    weights_hbm,
    modes_hbm,
    clocking_hbm,
    first_hbm,
    second_hbm,
    out,
    adj,
    layout,
    coupling,
    matching,
    weights,
    modes,
    clocking,
    first_j,
    second_j,
    pad,
    a_send,
    a_recv,
    full,
    terms,
    send1a,
    recv1a,
    stage1,
    send1b,
    recv1b,
    m_send,
    m_recv,
    swap,
    stage,
    send2,
    recv2,
    in_sem,
    j1_sem,
    j2_sem,
    a_ssem,
    a_rsem,
    s1a_sem,
    r1a_sem,
    s1b_sem,
    r1b_sem,
    m_ssem,
    m_rsem,
    s2_sem,
    r2_sem,
):
    my_t = lax.axis_index("tile")
    my_h = lax.axis_index("harm")
    own_hc, group, width = adj.shape
    rows, kk = first_j.shape[0], first_j.shape[1]
    hc = coupling.shape[0]
    half = hc // 2
    base = my_h * rows
    far = lax.rem(my_t + tiles // 2, tiles)
    near = [lax.rem(my_t + tiles - 1, tiles), my_t, lax.rem(my_t + 1, tiles)]

    barrier = pltpu.get_barrier_semaphore()
    for d in (-1, 0, 1):
        for h in range(harms):
            if d == 0:
                @pl.when(h != my_h)
                def _():
                    pl.semaphore_signal(barrier, inc=1, device_id=(my_t, h), device_id_type=MESH)
            else:
                pl.semaphore_signal(barrier, inc=1, device_id=(near[d + 1], h), device_id_type=MESH)
    for h in range(harms):
        pl.semaphore_signal(barrier, inc=1, device_id=(far, h), device_id_type=MESH)

    def block_copies(hbm, vmem, sem):
        return [
            pltpu.make_async_copy(hbm.at[r, k], vmem.at[r, k], sem.at[r * kk + k])
            for r in range(rows)
            for k in range(kk)
        ]

    first_copies = block_copies(first_hbm, first_j, j1_sem)
    second_copies = block_copies(second_hbm, second_j, j2_sem)
    pairs = [
        (adj_hbm, adj),
        (layout_hbm, layout),
        (coupling_hbm, coupling),
        (matching_hbm, matching),
        (weights_hbm, weights),
        (modes_hbm, modes),
        (clocking_hbm, clocking),
    ]
    in_copies = [
        pltpu.make_async_copy(src, dst, in_sem.at[i]) for i, (src, dst) in enumerate(pairs)
    ]
    for copy in in_copies:
        copy.start()
    for copy in first_copies:
        copy.start()

    pad[...] = jnp.zeros_like(pad)
    in_copies[0].wait()
    for h in range(harms):
        for r in range(rows):
            pad[h * rows + r, 0:own_hc, :] = adj[:, h * rows + r, :]
    for h in range(harms):
        for r in range(rows):
            a_send[h, r] = pad[h * rows + r].astype(jnp.bfloat16)

    pl.semaphore_wait(barrier, 4 * harms - 1)

    def a_copy(to, slot, sem):
        return pltpu.make_async_remote_copy(
            src_ref=a_send.at[to],
            dst_ref=a_recv.at[slot],
            send_sem=a_ssem.at[to],
            recv_sem=a_rsem.at[sem],
            device_id=(my_t, to),
            device_id_type=MESH,
        )

    def other(h):
        return h != my_h

    for h in range(harms):
        @pl.when(other(h))
        def _():
            a_copy(h, my_h, my_h).start()

    for copy in second_copies:
        copy.start()

    a_recv[my_h] = a_send[my_h]

    for copy in in_copies[1:]:
        copy.wait()
    row_id = lax.broadcasted_iota(jnp.int32, (hc, LANES), 0)
    lane_id = lax.broadcasted_iota(jnp.int32, (hc, LANES), 1)
    mode = jnp.zeros((hc, LANES), jnp.float32)
    for n in range(half):
        value = modes[n].astype(jnp.float32)
        mode = jnp.where((row_id == n) | (row_id == n + half), value, mode)
    cosines, sines = [], []
    for r in range(rows):
        phi = mode * clocking[base + r]
        inside = lane_id < STRIP
        sine = jnp.sin(phi)
        cosines.append(jnp.where(inside, jnp.cos(phi), 0.0))
        sines.append(jnp.where(inside, jnp.where(row_id < half, -sine, sine), 0.0))

    spot = [[layout[base + r, k] for k in range(kk)] for r in range(rows)]

    def one(r, k, slot):
        return jnp.where(spot[r][k] == slot, 1.0, 0.0).astype(jnp.float32)

    def fold(slot, low, high):
        total = None
        for r in range(rows):
            for k in range(kk):
                term = one(r, k, slot) * terms[r * kk + k, :, low:high]
                total = term if total is None else total + term
        return total

    for copy in first_copies:
        copy.wait()
    for h in range(harms):
        @pl.when(other(h))
        def _():
            a_copy(h, h, h).wait_recv()
    for r in range(rows):
        for h in range(harms):
            full[r, h * own_hc : (h + 1) * own_hc, :] = a_recv[h, r].astype(jnp.float32)[0:own_hc]

    def exchange(send, recv, ssem, rsem):
        def copy(d, to, slot):
            return pltpu.make_async_remote_copy(
                src_ref=send.at[(d + 1) * harms + to],
                dst_ref=recv.at[slot],
                send_sem=ssem.at[(d + 1) * harms + to],
                recv_sem=rsem.at[slot],
                device_id=(near[d + 1], to),
                device_id_type=MESH,
            )

        def start(d, to):
            if d == 0:
                @pl.when(other(to))
                def _():
                    copy(d, to, harms + my_h).start()
            else:
                copy(d, to, (d + 1) * harms + my_h).start()

        def finish(d, h):
            if d == 0:
                @pl.when(other(h))
                def _():
                    copy(d, h, harms + h).wait_recv()
            else:
                copy(d, h, (d + 1) * harms + h).wait_recv()

        def drain():
            for d in (-1, 0, 1):
                for h in range(harms):
                    if d == 0:
                        @pl.when(other(h))
                        def _():
                            copy(d, h, harms + h).wait_send()
                    else:
                        copy(d, h, (d + 1) * harms + h).wait_send()

        def collect(total):
            for d in (-1, 1, 0):
                for h in range(harms):
                    finish(d, h)
                if d == 0:
                    for j in range(1, harms):
                        slot = harms + lax.rem(my_h + j, harms)
                        total = total + recv[slot].astype(jnp.float32)
                else:
                    for h in range(harms):
                        total = total + recv[(d + 1) * harms + h].astype(jnp.float32)
            return total

        return start, collect, drain

    start1a, collect1a, drain1a = exchange(send1a, recv1a, s1a_sem, r1a_sem)
    start1b, collect1b, drain1b = exchange(send1b, recv1b, s1b_sem, r1b_sem)
    start2, collect2, drain2 = exchange(send2, recv2, s2_sem, r2_sem)

    vectors = [full[r].astype(jnp.bfloat16) for r in range(rows)]
    for low, high, send, start in ((0, LANES, send1a, start1a), (LANES, width, send1b, start1b)):
        for r in range(rows):
            for k in range(kk):
                terms[r * kk + k, :, low:high] = jnp.dot(
                    vectors[r],
                    first_j[r, k, :, low:high],
                    preferred_element_type=jnp.float32,
                )
        for d in (-1, 1, 0):
            for h in range(harms):
                for r in range(rows):
                    slot = (d + 1) * group + h * rows + r
                    if low == 0:
                        send[(d + 1) * harms + h, r] = fold(slot, low, high)
                    else:
                        stage1[r * hc : (r + 1) * hc, :] = fold(slot, low, high)
                if low > 0:
                    send[(d + 1) * harms + h] = stage1[...].astype(jnp.bfloat16)
                start(d, h)
    for r in range(rows):
        stage1[r * hc : (r + 1) * hc, :] = fold(group + my_h * rows + r, LANES, width)
    first_head = collect1a(send1a[harms + my_h])

    gap = LANES // rows
    assert gap >= STRIP
    packed = first_head[0]
    for r in range(1, rows):
        moved = pltpu.roll(first_head[r], r * gap, 1)
        packed = jnp.where(lane_id >= r * gap, moved, packed)
    m_send[...] = packed

    def m_copy(to, slot):
        return pltpu.make_async_remote_copy(
            src_ref=m_send,
            dst_ref=m_recv.at[slot],
            send_sem=m_ssem.at[to],
            recv_sem=m_rsem.at[slot],
            device_id=(far, to),
            device_id_type=MESH,
        )

    for h in range(harms):
        m_copy(h, my_h).start()

    def mix(part):
        mixed = jnp.dot(
            coupling[...],
            part,
            precision=lax.Precision.HIGHEST,
            preferred_element_type=jnp.float32,
        )
        return part + mixed

    plain_head = [mix(first_head[r]) for r in range(rows)]
    first_tail = collect1b(stage1[...])
    for copy in second_copies:
        copy.wait()
    for r in range(rows):
        tail = mix(first_tail[r * hc : (r + 1) * hc]).astype(jnp.bfloat16)
        for k in range(kk):
            terms[r * kk + k] = jnp.dot(
                tail, second_j[r, k, LANES:, :], preferred_element_type=jnp.float32
            )
    for h in range(harms):
        m_copy(h, h).wait_recv()
    for r in range(rows):
        mortar = jnp.zeros((hc, LANES), jnp.float32)
        for q in range(rows):
            part = jnp.zeros((hc, LANES), jnp.float32)
            for h in range(harms):
                place = h * rows + q
                weight = jnp.where(matching[0, base + r] == place, weights[0, base + r], 0.0)
                weight = weight + jnp.where(matching[1, base + r] == place, weights[1, base + r], 0.0)
                part = part + weight * m_recv[h]
            mortar = mortar + (part if q == 0 else pltpu.roll(part, LANES - q * gap, 1))
        swap[r, 0:half, :] = mortar[half:]
        swap[r, half:, :] = mortar[0:half]
        rotated = cosines[r] * mortar + sines[r] * swap[r]
        head = (plain_head[r] + rotated).astype(jnp.bfloat16)
        for k in range(kk):
            terms[r * kk + k] += jnp.dot(
                head, second_j[r, k, 0:LANES, :], preferred_element_type=jnp.float32
            )

    for d in (-1, 1, 0):
        for s in range(group):
            value = fold((d + 1) * group + s, 0, width)
            for h in range(harms):
                stage[h, s * own_hc : (s + 1) * own_hc, :] = value[
                    h * own_hc : (h + 1) * own_hc
                ]
        for h in range(harms):
            send2[(d + 1) * harms + h] = stage[h].astype(jnp.bfloat16)
            start2(d, h)
    second = collect2(stage[my_h])
    for s in range(group):
        out[:, s, :] = second[s * own_hc : (s + 1) * own_hc]

    for h in range(harms):
        @pl.when(other(h))
        def _():
            a_copy(h, h, h).wait_send()
        m_copy(h, h).wait_send()
    drain1a()
    drain1b()
    drain2()


def local(
    tiles,
    harms,
    adjoint,
    objective_grad,
    first_jacobian_blocks,
    second_jacobian_blocks,
    block_column_layout,
    coupling,
    matching,
    intersection,
    modes,
    clocking,
):
    own_hc, group, width = adjoint.shape
    rows, kk = first_jacobian_blocks.shape[:2]
    hc = coupling.shape[0]
    padded = -(-own_hc // 16) * 16
    vmem = pl.BlockSpec(memory_space=pltpu.VMEM)
    hbm = pl.BlockSpec(memory_space=pl.ANY)
    f32, bf16 = jnp.float32, jnp.bfloat16
    dma = pltpu.SemaphoreType.DMA
    second = pl.pallas_call(
        functools.partial(kernel, tiles, harms),
        out_shape=jax.ShapeDtypeStruct(objective_grad.shape, f32),
        in_specs=[hbm] * 9,
        out_specs=vmem,
        scratch_shapes=[
            pltpu.VMEM(adjoint.shape, f32),
            pltpu.SMEM(block_column_layout.shape, jnp.int32),
            pltpu.VMEM(coupling.shape, f32),
            pltpu.SMEM(matching.shape[::-1], jnp.int32),
            pltpu.SMEM(intersection.shape[::-1], f32),
            pltpu.SMEM(modes.shape, jnp.int32),
            pltpu.SMEM(clocking.shape, f32),
            pltpu.VMEM(first_jacobian_blocks.shape, bf16),
            pltpu.VMEM(first_jacobian_blocks.shape, bf16),
            pltpu.VMEM((group, padded, width), f32),
            pltpu.VMEM((harms, rows, padded, width), bf16),
            pltpu.VMEM((harms, rows, padded, width), bf16),
            pltpu.VMEM((rows, hc, width), f32),
            pltpu.VMEM((rows * kk, hc, width), f32),
            pltpu.VMEM((3 * harms, rows, hc, LANES), f32),
            pltpu.VMEM((3 * harms, rows, hc, LANES), f32),
            pltpu.VMEM((rows * hc, width - LANES), f32),
            pltpu.VMEM((3 * harms, rows * hc, width - LANES), bf16),
            pltpu.VMEM((3 * harms, rows * hc, width - LANES), bf16),
            pltpu.VMEM((hc, LANES), f32),
            pltpu.VMEM((harms, hc, LANES), f32),
            pltpu.VMEM((rows, hc, LANES), f32),
            pltpu.VMEM((harms, group * own_hc, width), f32),
            pltpu.VMEM((3 * harms, group * own_hc, width), bf16),
            pltpu.VMEM((3 * harms, group * own_hc, width), bf16),
            dma((7,)),
            dma((rows * kk,)),
            dma((rows * kk,)),
            dma((harms,)),
            dma((harms,)),
            dma((3 * harms,)),
            dma((3 * harms,)),
            dma((3 * harms,)),
            dma((3 * harms,)),
            dma((harms,)),
            dma((harms,)),
            dma((3 * harms,)),
            dma((3 * harms,)),
        ],
        compiler_params=pltpu.CompilerParams(
            collective_id=0, has_side_effects=True, vmem_limit_bytes=VMEM_BYTES
        ),
    )(
        adjoint,
        block_column_layout,
        coupling,
        matching.T,
        intersection.T,
        modes,
        clocking,
        first_jacobian_blocks,
        second_jacobian_blocks,
    )
    return objective_grad - second


def solution(mesh):
    return jax.shard_map(
        functools.partial(local, mesh.shape["tile"], mesh.shape["harm"]),
        mesh=mesh,
        in_specs=(
            P("harm", "tile", None),
            P("harm", "tile", None),
            P(("tile", "harm"), None, None, None),
            P(("tile", "harm"), None, None, None),
            P("tile", None),
            P(),
            P("tile", None),
            P("tile", None),
            P(),
            P("tile"),
        ),
        out_specs=P("harm", "tile", None),
        check_vma=False,
    )
```
